32 devices in a mesh: groups: 2 (over x), blk: 8 (over z, y), band: 2 (over core).
Axes of the slice: x: 2, y: 2, z: 4, core: 2. Of those that a mesh axis runs over, the one named last changes fastest.
Arguments:
- weights_slab: bfloat16 [6144, 3072], P(('groups', 'blk')), parts along dimension 0, may hold values from -2 to 2, as said below
- pairs: bfloat16 [512, 8, 3072], P(('groups', 'band'), None, 'blk'), parts along dimension 0, may hold values from -40 to 40
- occupation: int32 [512], P(('groups', 'band')), parts along dimension 0, may hold values 0 or 1
Outputs:
- screened: bfloat16 [512, 8, 3072], P(('groups', 'band'), None, 'blk'), parts along dimension 0
- sigma: float32 [16, 8], P('groups'), parts along dimension 0
The draws below stay inside these ranges and needn't reach their ends.
There are 2 independent parts, one for each index of `groups`. The reference program is written for one: setup_inputs(seed, part) draws one part's arguments, and reference() takes and returns one part's arrays. A program takes and returns all parts, laid end to end along the dimension named above; each array names one. Nothing has to cross between parts.
Inputs may be any that keep to these rules, and one draw needn't show every extreme that they name: weights_slab equals its transpose.
All inputs are finite; a program needn't handle non-finite values. No bound on the sum of `occupation` on one device may be relied on, other than what follows from the above.
Results may differ from the reference program's by a relative error of at most 0.0004.
Values may be sent and summed in bfloat16 or wider, within the bound.
No kernel may reach another device: no remote copies, remote signals or barrier semaphores. Data moves between devices by JAX's collectives and lax.ppermute only.
A program may use at most 128 MiB of HBM per device.

```python
import jax
import jax.numpy as jnp
from jax import lax

NB = 256
NQ = 8
SLAB = 3072


def draw_weights_slab(key, part):
    key = jax.random.fold_in(key, 11)
    first = jax.random.fold_in(key, 0)
    third = jax.random.fold_in(key, 2)
    base = jnp.clip(jax.random.normal(first, (SLAB, SLAB), jnp.float32), -6.0, 6.0)
    diagonal = jax.random.uniform(third, (SLAB,), jnp.float32, 0.5, 1.5)
    index = jnp.arange(SLAB)
    eye = (index[:, None] == index[None, :]).astype(jnp.float32)
    symmetric = (base + base.T) * (0.7071 / SLAB ** 0.5)
    symmetric = symmetric * (1.0 - eye)
    total = jnp.clip(symmetric + eye * diagonal[None, :], -1.98, 1.98)
    return total.astype(jnp.bfloat16)


def draw_pairs(key, part):
    key = jax.random.fold_in(key, 12)
    first, second = jax.random.split(key, 2)
    ramp = 3.0 ** (jnp.arange(SLAB).astype(jnp.float32) / SLAB)
    rough = jax.random.uniform(second, (SLAB,), jnp.float32, 0.5, 2.0)
    base = jnp.clip(jax.random.normal(first, (NB, NQ, SLAB), jnp.float32), -6.0, 6.0)
    return (base * ramp * rough).astype(jnp.bfloat16)


def plant(values, own_key, smallest, largest):
    longest = values.shape.index(max(values.shape))
    spots = []
    for shift in (0, 1):
        where = [jax.random.randint(jax.random.fold_in(own_key, axis), (), 0, length) for axis, length in enumerate(values.shape)]
        where[longest] = (where[longest] + shift) % values.shape[longest]
        spots.append(tuple(where))
    return values.at[spots[0]].set(smallest).at[spots[1]].set(largest)


def setup_inputs(seed: int = 0, part: int = 0) -> dict:
    splits = jax.random.split(jax.random.key(seed), 4)
    part_splits = jax.random.split(jax.random.fold_in(splits[3], part), 4)
    return {
        "weights_slab": draw_weights_slab(jax.random.fold_in(jax.random.fold_in(splits[3], part), 71), part),
        "pairs": draw_pairs(jax.random.fold_in(jax.random.fold_in(splits[3], part), 71), part),
        "occupation": plant((jax.random.randint(part_splits[2], (NB,), 0, 2) < 1).astype(jnp.int32), jax.random.fold_in(part_splits[2], 1), 0, 1),
    }


def reference(weights_slab, pairs, occupation):
    flat = pairs.reshape(NB * NQ, SLAB)
    wide = lax.dot_general(flat, weights_slab, (((1,), (1,)), ((), ())), preferred_element_type=jnp.float32)
    wide = wide.reshape(NB, NQ, SLAB)
    coeff = 0.5 - occupation.astype(jnp.float32)
    weighted = pairs.astype(jnp.float32) * coeff[:, None, None]
    sigma = jnp.einsum("bqg,bpg->qp", weighted, wide, precision=lax.Precision.HIGHEST) / (16.0 * SLAB)
    return wide.astype(jnp.bfloat16), sigma
```

```python
import jax
import jax.numpy as jnp
from jax import lax
from jax.sharding import PartitionSpec as P


def ring_order(n):
    if n == 8:
        return list(range(0, n, 2)) + list(range(n - 1, 0, -2))
    return list(range(n))


def pair_sum(x, axis, n):
    k = 1
    while k < n:
        x = x + lax.ppermute(x, axis, [(i, i ^ k) for i in range(n)])
        k *= 2
    return x


def local(weights_slab, pairs, occupation):
    nbands, nstates, rows = pairs.shape
    n = lax.axis_size("blk")
    order = ring_order(n)
    ring = jnp.array(order, jnp.int32)
    place = jnp.array([order.index(i) for i in range(n)], jnp.int32)[lax.axis_index("blk")]
    forth = [(order[i], order[(i + 1) % n]) for i in range(n)]
    back = [(b, a) for a, b in forth]
    flat = pairs.reshape(nbands * nstates, rows)
    half = nbands * nstates // 2
    parts = (flat[:half], flat[half:])

    def product(block, distance):
        owner = ring[(place + distance) % n]
        w = lax.dynamic_slice(weights_slab, (0, owner * rows), (rows, rows))
        return lax.dot_general(block, w, (((1,), (1,)), ((), ())), preferred_element_type=jnp.float32)

    acc = [product(parts[0], 0), product(parts[1], 0)]
    fw, bw = list(parts), list(parts)
    for step in range(1, n // 2 + 1):
        last = step == n // 2
        for h in (0, 1):
            if not last or h == 0:
                fw[h] = lax.ppermute(fw[h], "blk", forth)
            if not last or h == 0:
                bw[1 - h] = lax.ppermute(bw[1 - h], "blk", back)
        for h in (0, 1):
            if not last or h == 0:
                acc[h] = acc[h] + product(fw[h], -step)
                acc[1 - h] = acc[1 - h] + product(bw[1 - h], step)
    wide = jnp.concatenate(acc, axis=0)
    coeff = 0.5 - occupation.astype(jnp.float32)
    weighted = (pairs.astype(jnp.float32) * coeff[:, None, None]).astype(jnp.bfloat16).reshape(nbands * nstates, rows)
    rounded = lax.reduce_precision(wide, 8, 7)
    high = rounded.astype(jnp.bfloat16)
    low = (wide - rounded).astype(jnp.bfloat16)
    tile = 256
    gram = jnp.zeros((tile, tile), jnp.float32)
    for t in range(nbands * nstates // tile):
        s = slice(t * tile, (t + 1) * tile)
        for part in (high, low):
            gram = gram + lax.dot_general(weighted[s], part[s], (((1,), (1,)), ((), ())), preferred_element_type=jnp.float32)
    band = jnp.arange(tile) // nstates
    gram = jnp.where(band[:, None] == band[None, :], gram, 0.0)
    pick = (jnp.arange(tile)[:, None] % nstates == jnp.arange(nstates)[None, :]).astype(jnp.float32)
    folded = jnp.dot(gram, pick, precision=lax.Precision.HIGHEST)
    partial_sigma = jnp.dot(pick.T, folded, precision=lax.Precision.HIGHEST)
    sigma = pair_sum(pair_sum(partial_sigma, "band", lax.axis_size("band")), "blk", n) / (16.0 * rows * n)
    return (wide.astype(jnp.bfloat16).reshape(nbands, nstates, rows), sigma)


def solution(mesh):
    in_specs = (
        P(("groups", "blk"), None),
        P(("groups", "band"), None, "blk"),
        P(("groups", "band")),
    )
    out_specs = (P(("groups", "band"), None, "blk"), P("groups", None))
    return jax.shard_map(local, mesh=mesh, in_specs=in_specs, out_specs=out_specs, check_vma=False)
```

```python
import jax
import jax.numpy as jnp
from jax import lax
from jax.sharding import PartitionSpec as P

BEFORE = 0
BESIDE = 2
HOPS = [[1, 2, 3], [4]]


def ring_order(n):
    if n == 8:
        return list(range(0, n, 2)) + list(range(n - 1, 0, -2))
    return list(range(n))


def block_starts(n, depth):
    me = lax.axis_index("blk")
    if n != 8:
        return [(me + ahead) % n * depth for ahead in range(n)]
    place = jnp.where(me % 2 == 0, me // 2, n - 1 - me // 2)
    there = [(place + ahead) % n for ahead in range(n)]
    return [jnp.where(t < n // 2, 2 * t, 2 * (n - t) - 1) * depth for t in there]


def times(left, right):
    return lax.dot_general(left, right, (((1,), (1,)), ((), ())), preferred_element_type=jnp.float32)


def gram_of(weighted, halves, tile):
    gram = jnp.zeros((tile, tile), jnp.float32)
    row = 0
    for wide in halves:
        rounded = lax.reduce_precision(wide, 8, 7)
        parts = rounded.astype(jnp.bfloat16), (wide - rounded).astype(jnp.bfloat16)
        for t in range(0, wide.shape[0], tile):
            for part in parts:
                gram = gram + times(weighted[row : row + tile], part[t : t + tile])
            row += tile
    return gram


def band_sums(gram, nstates):
    tile = gram.shape[0]
    band = jnp.arange(tile) // nstates
    gram = jnp.where(band[:, None] == band[None, :], gram, 0.0)
    pick = (jnp.arange(tile)[:, None] % nstates == jnp.arange(nstates)[None, :]).astype(jnp.float32)
    folded = jnp.dot(gram, pick, precision=lax.Precision.HIGHEST)
    return jnp.dot(pick.T, folded, precision=lax.Precision.HIGHEST)


def local(weights_slab, pairs, occupation):
    nbands, nstates, depth = pairs.shape
    rows = nbands * nstates
    n = lax.axis_size("blk")
    half = n // 2
    order = ring_order(n)
    forth = [(order[i], order[(i + 1) % n]) for i in range(n)]
    back = [(b, a) for a, b in forth]
    starts = block_starts(n, depth)
    flat = pairs.reshape(rows, depth)
    upper, lower = slice(0, rows // 2), slice(rows // 2, rows)
    together = lax.optimization_barrier

    def product(block, distance):
        return times(block, lax.dynamic_slice(weights_slab, (0, starts[distance % n]), (depth, depth)))

    def move(pair, ways):
        return [lax.ppermute(block, "blk", way) for block, way in zip(pair, ways)]

    came_forth, came_back = move([flat, flat], (forth, back))
    own = [product(flat[upper], 0), product(flat[lower], 0)]
    coeff = 0.5 - occupation.astype(jnp.float32)
    weighted = (pairs.astype(jnp.float32) * coeff[:, None, None]).astype(jnp.bfloat16).reshape(rows, depth)
    came_forth, came_back, own, weighted = together((came_forth, came_back, own, weighted))

    block, late = [came_forth[upper], came_back[lower]], [came_back[upper], came_forth[lower]]
    near = [0.5 * own[0] + product(block[0], -1), 0.5 * own[1] + product(block[1], 1)]
    rest = [0.5 * own[0] + product(late[0], 1), 0.5 * own[1] + product(late[1], -1)]
    for step in range(2, half):
        block = move(block, (forth, back))
        if step > 3:
            late = move(late, (back, forth))
        block, late, near, rest = together((block, late, near, rest))
        near = [near[0] + product(block[0], -step), near[1] + product(block[1], step)]
        if step > 3:
            rest = [rest[0] + product(late[0], step - 2), rest[1] + product(late[1], 2 - step)]

    hops = [("band", [1])] + [("blk", k) for k in HOPS] + [("blk", [1 << k]) for k in range(3, n.bit_length() - 1)]

    def exchange(share, count):
        for _ in range(count):
            axis, offsets = hops.pop(0)
            size = lax.axis_size(axis)
            share = sum([lax.ppermute(share, axis, [(i, i ^ k) for i in range(size)]) for k in offsets], share)
        return share

    far = move(block, (forth, back))
    late = move(late, (back, forth))
    gram = gram_of(weighted, near, rows // 4)
    rest = [near[h] + rest[h] for h in (0, 1)]
    far = [product(far[h], half) for h in (0, 1)]
    share = band_sums(gram + gram_of(weighted, [0.5 * f for f in far], rows // 4), nstates)
    rest = [rest[h] + far[h] for h in (0, 1)]
    share = exchange(share, BEFORE)
    late, share, rest = together((late, share, rest))
    rest = [rest[0] + product(late[0], half - 2), rest[1] + product(late[1], 2 - half)]
    late = move(late, (back, forth))
    share = exchange(share, BESIDE)
    late, share, rest = together((late, share, rest))
    rest = [rest[0] + product(late[0], half - 1), rest[1] + product(late[1], 1 - half)]
    share = exchange(share, len(hops))
    sigma = (share + share.T) / (16.0 * depth * n)
    wide = jnp.concatenate(rest, axis=0)
    return (wide.astype(jnp.bfloat16).reshape(nbands, nstates, depth), sigma)


def solution(mesh):
    in_specs = (
        P(("groups", "blk"), None),
        P(("groups", "band"), None, "blk"),
        P(("groups", "band")),
    )
    out_specs = (P(("groups", "band"), None, "blk"), P("groups", None))
    return jax.shard_map(local, mesh=mesh, in_specs=in_specs, out_specs=out_specs, check_vma=False)
```

```python
import jax
import jax.numpy as jnp
from jax import lax
from jax.sharding import PartitionSpec as P


def ring_order(n):
    if n == 8:
        return list(range(0, n, 2)) + list(range(n - 1, 0, -2))
    return list(range(n))


def block_starts(n, depth):
    me = lax.axis_index("blk")
    if n != 8:
        return [(me + ahead) % n * depth for ahead in range(n)]
    place = jnp.where(me % 2 == 0, me // 2, n - 1 - me // 2)
    there = [(place + ahead) % n for ahead in range(n)]
    return [jnp.where(t < n // 2, 2 * t, 2 * (n - t) - 1) * depth for t in there]


def times(left, right):
    return lax.dot_general(left, right, (((1,), (1,)), ((), ())), preferred_element_type=jnp.float32)


def two_terms(x):
    rounded = lax.reduce_precision(x, 8, 7)
    return rounded.astype(jnp.bfloat16), (x - rounded).astype(jnp.bfloat16)


def gram_of(left, right, tile):
    cuts = [slice(t, t + tile) for t in range(0, left.shape[0], tile)]
    return sum(times(left[s], right[s]) for s in cuts)


def band_sums(gram, nstates):
    tile = gram.shape[0]
    band = jnp.arange(tile) // nstates
    gram = jnp.where(band[:, None] == band[None, :], gram, 0.0)
    pick = (jnp.arange(tile)[:, None] % nstates == jnp.arange(nstates)[None, :]).astype(jnp.float32)
    folded = jnp.dot(gram, pick, precision=lax.Precision.HIGHEST)
    return jnp.dot(pick.T, folded, precision=lax.Precision.HIGHEST)


def local(weights_slab, pairs, occupation):
    nbands, nstates, depth = pairs.shape
    rows = nbands * nstates
    n = lax.axis_size("blk")
    half = n // 2
    order = ring_order(n)
    forth = [(order[i], order[(i + 1) % n]) for i in range(n)]
    back = [(b, a) for a, b in forth]
    starts = block_starts(n, depth)
    flat = pairs.reshape(rows, depth)
    upper, lower = slice(0, rows // 2), slice(rows // 2, rows)
    together = lax.optimization_barrier

    def product(block, distance):
        return times(block, lax.dynamic_slice(weights_slab, (0, starts[distance % n]), (depth, depth)))

    def move(pair, ways):
        return [lax.ppermute(block, "blk", way) for block, way in zip(pair, ways)]

    came_forth, came_back = move([flat, flat], (forth, back))
    own = [product(flat[upper], 0), product(flat[lower], 0)]
    coeff = 0.5 - occupation.astype(jnp.float32)
    weighted = (pairs.astype(jnp.float32) * coeff[:, None, None]).astype(jnp.bfloat16).reshape(rows, depth)
    opposite = lax.dynamic_slice(weights_slab, (0, starts[half]), (depth, depth))
    across = lax.dot_general(weighted, opposite, (((1,), (0,)), ((), ())), preferred_element_type=jnp.float32)
    across = two_terms(0.5 * across)
    came_forth, came_back, own, weighted, across = together((came_forth, came_back, own, weighted, across))

    block, late = [came_forth[upper], came_back[lower]], [came_back[upper], came_forth[lower]]
    near = [0.5 * own[0] + product(block[0], -1), 0.5 * own[1] + product(block[1], 1)]
    rest = [0.5 * own[0] + product(late[0], 1), 0.5 * own[1] + product(late[1], -1)]
    for step in range(2, half):
        block = move(block, (forth, back))
        if step > 3:
            late = move(late, (back, forth))
        block, late, near, rest = together((block, late, near, rest))
        near = [near[0] + product(block[0], -step), near[1] + product(block[1], step)]
        if step > 3:
            rest = [rest[0] + product(late[0], step - 2), rest[1] + product(late[1], 2 - step)]

    hops = [("blk", k) for k in ([1, 2, 3], [4])] + [("blk", [1 << k]) for k in range(3, n.bit_length() - 1)]
    hops.insert(2, ("band", [1]))

    def exchange(share, count):
        for _ in range(count):
            axis, offsets = hops.pop(0)
            size = lax.axis_size(axis)
            share = sum([lax.ppermute(share, axis, [(i, i ^ k) for i in range(size)]) for k in offsets], share)
        return share

    tile = rows // 4
    far = move(block, (forth, back))
    gram = 0.0
    for h, side in enumerate((upper, lower)):
        gram = gram + sum(gram_of(weighted[side], part, tile) for part in two_terms(near[h]))
    late, gram = together((late, gram))
    late = move(late, (back, forth))
    gram, far = together((gram, far))
    for h, side in enumerate((upper, lower)):
        gram = gram + sum(gram_of(part[side], far[h], tile) for part in across)
    share = band_sums(gram, nstates)
    rest = [near[h] + rest[h] for h in (0, 1)]
    far = [product(far[h], half) for h in (0, 1)]
    rest = [rest[h] + far[h] for h in (0, 1)]
    late, share, rest = together((late, share, rest))
    rest = [rest[0] + product(late[0], half - 2), rest[1] + product(late[1], 2 - half)]
    late = move(late, (back, forth))
    share = exchange(share, 2)
    late, share, rest = together((late, share, rest))
    rest = [rest[0] + product(late[0], half - 1), rest[1] + product(late[1], 1 - half)]
    share = exchange(share, len(hops))
    sigma = (share + share.T) / (16.0 * depth * n)
    wide = jnp.concatenate(rest, axis=0)
    return (wide.astype(jnp.bfloat16).reshape(nbands, nstates, depth), sigma)


def solution(mesh):
    in_specs = (
        P(("groups", "blk"), None),
        P(("groups", "band"), None, "blk"),
        P(("groups", "band")),
    )
    out_specs = (P(("groups", "band"), None, "blk"), P("groups", None))
    return jax.shard_map(local, mesh=mesh, in_specs=in_specs, out_specs=out_specs, check_vma=False)
```

```python
import jax
import jax.numpy as jnp
from jax import lax
from jax.sharding import PartitionSpec as P


def ring_order(n):
    if n == 8:
        return list(range(0, n, 2)) + list(range(n - 1, 0, -2))
    return list(range(n))


def block_starts(n, depth):
    me = lax.axis_index("blk")
    if n != 8:
        return [(me + ahead) % n * depth for ahead in range(n)]
    place = jnp.where(me % 2 == 0, me // 2, n - 1 - me // 2)
    there = [(place + ahead) % n for ahead in range(n)]
    return [jnp.where(t < n // 2, 2 * t, 2 * (n - t) - 1) * depth for t in there]


def times(left, right):
    return lax.dot_general(left, right, (((1,), (1,)), ((), ())), preferred_element_type=jnp.float32)


def two_terms(x):
    rounded = lax.reduce_precision(x, 8, 7)
    return rounded.astype(jnp.bfloat16), (x - rounded).astype(jnp.bfloat16)


def gram_of(left, right, tile):
    cuts = [slice(t, t + tile) for t in range(0, left.shape[0], tile)]
    return sum(times(left[s], right[s]) for s in cuts)


def band_sums(gram, nstates):
    tile = gram.shape[0]
    band = jnp.arange(tile) // nstates
    gram = jnp.where(band[:, None] == band[None, :], gram, 0.0)
    pick = (jnp.arange(tile)[:, None] % nstates == jnp.arange(nstates)[None, :]).astype(jnp.float32)
    folded = jnp.dot(gram, pick, precision=lax.Precision.HIGHEST)
    return jnp.dot(pick.T, folded, precision=lax.Precision.HIGHEST)


def local(weights_slab, pairs, occupation):
    nbands, nstates, depth = pairs.shape
    rows = nbands * nstates
    n = lax.axis_size("blk")
    half = n // 2
    order = ring_order(n)
    forth = [(order[i], order[(i + 1) % n]) for i in range(n)]
    back = [(b, a) for a, b in forth]
    starts = block_starts(n, depth)
    flat = pairs.reshape(rows, depth)
    upper, lower = slice(0, rows // 2), slice(rows // 2, rows)
    together = lax.optimization_barrier

    def product(block, distance):
        return times(block, lax.dynamic_slice(weights_slab, (0, starts[distance % n]), (depth, depth)))

    def move(pair, ways):
        return [lax.ppermute(block, "blk", way) for block, way in zip(pair, ways)]

    came_forth, came_back = move([flat, flat], (forth, back))
    own = [product(flat[upper], 0), product(flat[lower], 0)]
    coeff = 0.5 - occupation.astype(jnp.float32)
    weighted = (pairs.astype(jnp.float32) * coeff[:, None, None]).astype(jnp.bfloat16).reshape(rows, depth)
    opposite = lax.dynamic_slice(weights_slab, (0, starts[half]), (depth, depth))
    across = lax.dot_general(weighted, opposite, (((1,), (0,)), ((), ())), preferred_element_type=jnp.float32)
    across = two_terms(0.5 * across)
    came_forth, came_back, own, weighted, across = together((came_forth, came_back, own, weighted, across))

    block, came, late = [came_forth[upper], came_back[lower]], (came_back, came_forth), None
    near = [0.5 * own[0] + product(block[0], -1), 0.5 * own[1] + product(block[1], 1)]
    rest = [0.5 * o for o in own]
    for step in range(2, half):
        block = move(block, (forth, back))
        if step > 3:
            late = move(late, (back, forth))
        block, late, near, rest, came = together((block, late, near, rest, came))
        if step == 2:
            late = [came[0][upper], came[1][lower]]
            rest = [rest[0] + product(late[0], 1), rest[1] + product(late[1], -1)]
        near = [near[0] + product(block[0], -step), near[1] + product(block[1], step)]
        if step > 3:
            rest = [rest[0] + product(late[0], step - 2), rest[1] + product(late[1], 2 - step)]

    hops = [("blk", k) for k in ([1, 2, 3], [4])] + [("blk", [1 << k]) for k in range(3, n.bit_length() - 1)]
    hops.insert(2, ("band", [1]))

    def exchange(share, count):
        for _ in range(count):
            axis, offsets = hops.pop(0)
            size = lax.axis_size(axis)
            share = sum([lax.ppermute(share, axis, [(i, i ^ k) for i in range(size)]) for k in offsets], share)
        return share

    tile = rows // 4
    far = move(block, (forth, back))
    gram = 0.0
    for h, side in enumerate((upper, lower)):
        gram = gram + sum(gram_of(weighted[side], part, tile) for part in two_terms(near[h]))
    late, gram = together((late, gram))
    late = move(late, (back, forth))
    gram, far = together((gram, far))
    for h, side in enumerate((upper, lower)):
        gram = gram + sum(gram_of(part[side], far[h], tile) for part in across)
    share = band_sums(gram, nstates)
    rest = [near[h] + rest[h] for h in (0, 1)]
    far = [product(far[h], half) for h in (0, 1)]
    rest = [rest[h] + far[h] for h in (0, 1)]
    late, rest = together((late, rest))
    rest = [rest[0] + product(late[0], half - 2), rest[1] + product(late[1], 2 - half)]
    late = move(late, (back, forth))
    share = exchange(share, 2)
    late, share, rest = together((late, share, rest))
    rest = [rest[0] + product(late[0], half - 1), rest[1] + product(late[1], 1 - half)]
    share = exchange(share, len(hops))
    sigma = (share + share.T) / (16.0 * depth * n)
    wide = jnp.concatenate(rest, axis=0)
    return (wide.astype(jnp.bfloat16).reshape(nbands, nstates, depth), sigma)


def solution(mesh):
    in_specs = (
        P(("groups", "blk"), None),
        P(("groups", "band"), None, "blk"),
        P(("groups", "band")),
    )
    out_specs = (P(("groups", "band"), None, "blk"), P("groups", None))
    return jax.shard_map(local, mesh=mesh, in_specs=in_specs, out_specs=out_specs, check_vma=False)
```

```python
import jax
import jax.numpy as jnp
from jax import lax
from jax.sharding import PartitionSpec as P


def ring_order(n):
    if n == 8:
        return list(range(0, n, 2)) + list(range(n - 1, 0, -2))
    return list(range(n))


def block_starts(n, depth):
    me = lax.axis_index("blk")
    if n != 8:
        return [(me + ahead) % n * depth for ahead in range(n)]
    place = jnp.where(me % 2 == 0, me // 2, n - 1 - me // 2)
    there = [(place + ahead) % n for ahead in range(n)]
    return [jnp.where(t < n // 2, 2 * t, 2 * (n - t) - 1) * depth for t in there]


def times(left, right):
    return lax.dot_general(left, right, (((1,), (1,)), ((), ())), preferred_element_type=jnp.float32)


def two_terms(x):
    rounded = lax.reduce_precision(x, 8, 7)
    return rounded.astype(jnp.bfloat16), (x - rounded).astype(jnp.bfloat16)


def gram_of(left, right, tile):
    cuts = [slice(t, t + tile) for t in range(0, left.shape[0], tile)]
    return sum(times(left[s], right[s]) for s in cuts)


def band_sums(gram, nstates):
    tile = gram.shape[0]
    band = jnp.arange(tile) // nstates
    gram = jnp.where(band[:, None] == band[None, :], gram, 0.0)
    pick = (jnp.arange(tile)[:, None] % nstates == jnp.arange(nstates)[None, :]).astype(jnp.float32)
    folded = jnp.dot(gram, pick, precision=lax.Precision.HIGHEST)
    return jnp.dot(pick.T, folded, precision=lax.Precision.HIGHEST)


def local(weights_slab, pairs, occupation):
    nbands, nstates, depth = pairs.shape
    rows = nbands * nstates
    n = lax.axis_size("blk")
    half = n // 2
    order = ring_order(n)
    forth = [(order[i], order[(i + 1) % n]) for i in range(n)]
    back = [(b, a) for a, b in forth]
    starts = block_starts(n, depth)
    flat = pairs.reshape(rows, depth)
    upper, lower = slice(0, rows // 2), slice(rows // 2, rows)
    together = lax.optimization_barrier

    def product(block, distance):
        return times(block, lax.dynamic_slice(weights_slab, (0, starts[distance % n]), (depth, depth)))

    def move(pair, ways):
        return [lax.ppermute(block, "blk", way) for block, way in zip(pair, ways)]

    came_forth, came_back = move([flat, flat], (forth, back))
    own = [product(flat[upper], 0), product(flat[lower], 0)]
    coeff = 0.5 - occupation.astype(jnp.float32)
    weighted = (pairs.astype(jnp.float32) * coeff[:, None, None]).astype(jnp.bfloat16).reshape(rows, depth)
    opposite = lax.dynamic_slice(weights_slab, (0, starts[half]), (depth, depth))
    across = lax.dot_general(weighted, opposite, (((1,), (0,)), ((), ())), preferred_element_type=jnp.float32)
    across = two_terms(0.5 * across)
    came_forth, came_back, across = together((came_forth, came_back, across))

    block, came, late = [came_forth[upper], came_back[lower]], (came_back, came_forth), None
    near = [0.5 * own[0] + product(block[0], -1), 0.5 * own[1] + product(block[1], 1)]
    rest = [0.5 * o for o in own]
    for step in range(2, half):
        block = move(block, (forth, back))
        if step > 3:
            late = move(late, (back, forth))
        block, late, near, rest, came = together((block, late, near, rest, came))
        if step == 2:
            late = [came[0][upper], came[1][lower]]
            rest = [rest[0] + product(late[0], 1), rest[1] + product(late[1], -1)]
        near = [near[0] + product(block[0], -step), near[1] + product(block[1], step)]
        if step > 3:
            rest = [rest[0] + product(late[0], step - 2), rest[1] + product(late[1], 2 - step)]

    hops = [("blk", k) for k in ([1, 2, 3], [4])] + [("blk", [1 << k]) for k in range(3, n.bit_length() - 1)]
    hops.insert(2, ("band", [1]))

    def exchange(share, count):
        for _ in range(count):
            axis, offsets = hops.pop(0)
            size = lax.axis_size(axis)
            share = sum([lax.ppermute(share, axis, [(i, i ^ k) for i in range(size)]) for k in offsets], share)
        return share

    tile = rows // 4
    far = move(block, (forth, back))
    gram = 0.0
    for h, side in enumerate((upper, lower)):
        gram = gram + sum(gram_of(weighted[side], part, tile) for part in two_terms(near[h]))
    late, gram = together((late, gram))
    late = move(late, (back, forth))
    gram, far = together((gram, far))
    for h, side in enumerate((upper, lower)):
        gram = gram + sum(gram_of(part[side], far[h], tile) for part in across)
    share = band_sums(gram, nstates)
    rest = [near[h] + rest[h] for h in (0, 1)]
    far = [product(far[h], half) for h in (0, 1)]
    rest = [rest[h] + far[h] for h in (0, 1)]
    rest = [rest[0] + product(late[0], half - 2), rest[1] + product(late[1], 2 - half)]
    late = move(late, (back, forth))
    share = exchange(share, 2)
    late, share, rest = together((late, share, rest))
    rest = [rest[0] + product(late[0], half - 1), rest[1] + product(late[1], 1 - half)]
    share = exchange(share, len(hops))
    sigma = (share + share.T) / (16.0 * depth * n)
    wide = jnp.concatenate(rest, axis=0)
    return (wide.astype(jnp.bfloat16).reshape(nbands, nstates, depth), sigma)


def solution(mesh):
    in_specs = (
        P(("groups", "blk"), None),
        P(("groups", "band"), None, "blk"),
        P(("groups", "band")),
    )
    out_specs = (P(("groups", "band"), None, "blk"), P("groups", None))
    return jax.shard_map(local, mesh=mesh, in_specs=in_specs, out_specs=out_specs, check_vma=False)
```
